32 devices in a mesh: dp: 4 (over z), ep: 8 (over y, x, core).
Axes of the slice: x: 2, y: 2, z: 4, core: 2. Of those that a mesh axis runs over, the one named last changes fastest.
Arguments:
- queries: bfloat16 [512, 2, 8192], P(('dp', 'ep')), may hold values from -150 to 150
- keys_new: bfloat16 [512, 2, 512], P(('dp', 'ep')), may hold values from -5 to 5
- values_new: bfloat16 [512, 2, 512], P(('dp', 'ep')), may hold values from -5 to 5
- importance: float32 [512, 2, 4], P(('dp', 'ep')), may hold values from 0.25 to 4
- merge_flags: int32 [512, 2, 4], P(('dp', 'ep')), may hold values 0 or 1
- key_cache: bfloat16 [512, 512, 512], P(('dp', 'ep')), may hold values from -5.1 to 5.1
- value_cache: bfloat16 [512, 512, 512], P(('dp', 'ep')), may hold values from -5 to 5
- last_weight: float32 [512, 4], P(('dp', 'ep')), may hold values from 0.5 to 8
- lengths: int32 [512], P(('dp', 'ep')), may hold values from 2 to 510, as said below
- residual: bfloat16 [512, 2, 2048], P(('dp', 'ep')), may hold values from -6 to 6
- o_weight: bfloat16 [8192, 2048], P('ep'), may hold values from -0.0625 to 0.0625
- norm_gain: float32 [2048], replicated, may hold values from 0.5 to 1.5
- expert_gate_up: bfloat16 [32, 2048, 1536], P(('dp', 'ep')), may hold values from -0.125 to 0.125
- expert_down: bfloat16 [32, 768, 2048], P(('dp', 'ep')), may hold values from -0.21875 to 0.21875
- routes: int32 [512, 2, 8], P(('dp', 'ep')), may hold values from 0 to 31, all different within a row; in each aligned block of 32 rows (0 to 31, 32 to 63, ..., all dimensions but the last counted through in order) at most 16 rows name the same one
- route_weights: float32 [512, 2, 8], P(('dp', 'ep')), may hold values from 0.05 to 0.5
Outputs:
- attended: bfloat16 [512, 2, 8192], P(('dp', 'ep'))
- layer_out: bfloat16 [512, 2, 2048], P(('dp', 'ep'))
The draws below stay inside these ranges and needn't reach their ends.
Inputs may be any that keep to these rules, and one draw needn't show every extreme that they name: `lengths`: the largest length is 510 in every draw. `routes`: each token names 8 different experts; among the rows of one device (32 tokens) no expert is named more than 16 times, a bound that some block reaches.
All inputs are finite; a program needn't handle non-finite values. No bound on the sum of `merge_flags` on one device may be relied on, other than what follows from the above.
Results may differ from the reference program's by a relative error of at most 0.018.
Values may be sent and summed in bfloat16 or wider, within the bound.
A program may use at most 128 MiB of HBM per device.

```python
import math
import jax
import jax.numpy as jnp
import numpy as np
from jax import lax

D = 2048
QH = 64
KVH = 4
HD = 128
FF = 768
TOPK = 8
STEPS = 2
R_DEV = 16
CAP = 512
EXPERTS = 32
REQ = 512
CAPE = 16
N_DP = 4
N_EP = 8


def first_keys(key):
    return jax.random.truncated_normal(jax.random.fold_in(key, 12), -5.0, 5.0, (REQ, KVH * HD), jnp.float32)


def draw_key_cache(key, part):
    rest = jax.random.truncated_normal(jax.random.fold_in(key, 13), -5.0, 5.0, (REQ, CAP, KVH * HD), jnp.float32)
    first = first_keys(key)
    rest = rest.at[:, 0].set(first)
    return rest.astype(jnp.bfloat16)


def draw_queries(key, part):
    base = jax.random.truncated_normal(jax.random.fold_in(key, 14), -5.0, 5.0, (REQ, STEPS, QH * HD), jnp.float32)
    return base.astype(jnp.bfloat16)


def draw_lengths(key, part):
    first, second, third, fourth = jax.random.split(key, 4)
    short_lengths = jax.random.randint(first, (REQ,), 2, max(3, CAP // 8))
    long_lengths = jax.random.randint(second, (REQ,), CAP // 2, CAP - STEPS + 1)
    picked = jax.random.randint(third, (REQ,), 0, 8) == 0
    result = jnp.where(picked, long_lengths, short_lengths)
    longest = jax.random.randint(fourth, (), 0, REQ)
    return result.at[longest].set(CAP - STEPS).astype(jnp.int32)


def plant(array, own_key, smallest, largest):
    dims = array.shape
    place = [jax.random.randint(jax.random.fold_in(own_key, axis), (), 0, dims[axis]) for axis in range(len(dims))]
    array = array.at[tuple(place)].set(smallest)
    longest = dims.index(max(dims))
    place[longest] = (place[longest] + 1) % dims[longest]
    return array.at[tuple(place)].set(largest)


def levels(stream_key, extent, cuts, least, top_value):
    def one(position, parts):
        steps = jax.random.uniform(jax.random.fold_in(jax.random.fold_in(stream_key, 6), position), (parts,), jnp.float32, least / len(cuts), top_value / len(cuts))
        return jnp.repeat(jnp.exp(steps), extent[position] // parts).reshape((-1,) + (1,) * (len(extent) - position - 1))

    gain = one(*cuts[0])
    for cut in cuts[1:]:
        gain = gain * one(*cut)
    return gain


def shared_out(rng, own, number, rows, count, top, reach, lean):
    order = jax.random.permutation(rng, count)
    heavy_load, usual = portions_of(count, rows * top, reach, lean, True), portions_of(count, rows * top, reach, lean, False)
    places = jnp.arange(count)

    def named(sizes, turn):
        used = int((sizes > 0).sum())
        fixed = max(1, used // 4)
        moved = fixed + (places - fixed + turn * (used - fixed)) % max(1, count - fixed)
        return jnp.zeros((count,), jnp.int32).at[order[jnp.where(places < fixed, places, moved)]].set(jnp.asarray(sizes, jnp.int32))

    sizes = jnp.where(number % 4 == 0, named(heavy_load, number // 4), named(usual, number - number // 4 - 1))
    mixed = jax.random.permutation(jax.random.fold_in(own, 3), count)
    giver, receiver = mixed[0:count // 2 * 2:2], mixed[1:count // 2 * 2:2]
    margin = jnp.minimum(sizes[giver] - 1, reach - sizes[receiver]) // 2
    margin = jnp.where((giver == order[0]) | (receiver == order[0]) | (sizes[receiver] == 0), 0, jnp.maximum(margin, 0))
    moved = jax.random.randint(jax.random.fold_in(own, 4), (count // 2,), 0, 1 << 20) % (margin + 1)
    sizes = sizes.at[giver].add(-moved).at[receiver].add(moved)
    members = jnp.searchsorted(jnp.cumsum(sizes), jnp.arange(rows * top), side="right").astype(jnp.int32)
    grid = members.reshape(top, rows).T
    grid = grid[jax.random.permutation(jax.random.fold_in(own, 1), rows)]
    turn = jax.random.randint(jax.random.fold_in(own, 2), (rows, 1), 0, top)
    return jnp.take_along_axis(grid, (jnp.arange(top)[None, :] + turn) % top, axis=1)


def portions_of(count, total, reach, slope, full):
    loads = [(1 << 20) // math.isqrt(rank ** slope) + 1 for rank in range(1, count + 1)]
    largest = reach if full else min(reach, max(-(-total // count), total * loads[0] // sum(loads)))
    least = 1 if total - largest >= count - 1 else 0
    given, spare = [largest] + [least] * (count - 1), total - largest - least * (count - 1)
    while spare > 0:
        movable = [i for i in range(1, count) if given[i] < largest] or [i for i in range(1, count) if given[i] < reach]
        pool, left = sum([loads[i] for i in movable]), spare
        for i in movable:
            more = min(reach - given[i], max(1, left * loads[i] // pool), spare)
            given[i] = given[i] + more
            spare = spare - more
    return np.array(given)


def scatter_about(key, shape, width, reach, shards=(), kind=jnp.bfloat16):
    values = jax.random.normal(key, shape, jnp.float32) * width
    if len(shards) > 0:
        values = levels(key, shape, shards, -0.22, 0.18) * values
    return jnp.clip(values, min=-reach, max=reach).astype(kind)


def setup_inputs(seed: int = 0) -> dict:
    seeds = jax.random.split(jax.random.key(seed), 17)
    queries = draw_queries(jax.random.fold_in(seeds[16], 71), 0)
    keys_new = scatter_about(seeds[1], (REQ, STEPS, KVH * HD), 1.0, 5.0, ((0, 32),))
    values_new = scatter_about(seeds[2], (REQ, STEPS, KVH * HD), 1.0, 5.0, ((0, 32),))
    importance = jnp.clip(jnp.exp(math.log(4.0) - 2.7725887 * jax.random.uniform(seeds[3], (REQ, STEPS, KVH), jnp.float32) ** levels(seeds[3], (REQ, STEPS, KVH), ((0, 32),), -0.2, 0.2)), 0.25, 4.0)
    merge_flags = plant((jax.random.randint(seeds[4], (REQ, STEPS, KVH), 0, 4) < 3).astype(jnp.int32), jax.random.fold_in(seeds[4], 1), 0, 1)
    key_cache = draw_key_cache(jax.random.fold_in(seeds[16], 71), 0)
    value_cache = scatter_about(seeds[6], (REQ, CAP, KVH * HD), 1.0, 5.0, ((0, 32),))
    last_weight = jnp.clip(jnp.exp(math.log(8.0) - 2.7725887 * jax.random.uniform(seeds[7], (REQ, KVH), jnp.float32) ** levels(seeds[7], (REQ, KVH), ((0, 32),), -0.2, 0.2)), 0.5, 8.0)
    lengths = draw_lengths(jax.random.fold_in(seeds[16], 71), 0)
    residual = scatter_about(seeds[9], (REQ, STEPS, D), 1.0, 6.0, ((0, 32),))
    o_weight = scatter_about(seeds[10], (QH * HD, D), (QH * HD) ** -0.5, 0.0625, ((0, 8),))
    norm_gain = jnp.clip(1.0 + 0.1 * jax.random.normal(seeds[11], (D,), jnp.float32), 0.5, 1.5)
    expert_gate_up = scatter_about(seeds[12], (EXPERTS, D, 2 * FF), D ** -0.5, 0.125, ((0, 32),))
    expert_down = scatter_about(seeds[13], (EXPERTS, FF, D), FF ** -0.5, 0.21875, ((0, 32),))
    routes_keys = jax.random.split(jax.random.fold_in(seeds[14], 1), REQ * STEPS // (R_DEV * STEPS))
    routes_turns = jax.random.permutation(jax.random.fold_in(seeds[14], 3), REQ * STEPS // (R_DEV * STEPS))
    routes = jax.vmap(lambda own, number: shared_out(jax.random.fold_in(seeds[14], 2), own, number, R_DEV * STEPS, EXPERTS, TOPK, CAPE, 2))(routes_keys, routes_turns).reshape((REQ, STEPS, TOPK))
    route_weights = jnp.clip(jnp.exp(math.log(0.5) - 2.3025851 * jax.random.uniform(seeds[15], (REQ, STEPS, TOPK), jnp.float32) ** levels(seeds[15], (REQ, STEPS, TOPK), ((0, 32),), -0.2, 0.2)), 0.05, 0.5)
    return dict(queries=queries, keys_new=keys_new, values_new=values_new, importance=importance, merge_flags=merge_flags, key_cache=key_cache, value_cache=value_cache, last_weight=last_weight, lengths=lengths, residual=residual, o_weight=o_weight, norm_gain=norm_gain, expert_gate_up=expert_gate_up, expert_down=expert_down, routes=routes, route_weights=route_weights)


EPS = 1e-06

def one_request(query_rows, fresh_keys, fresh_values, shares, flags, key_rows, value_rows, weight, length):
    group = QH // KVH
    scale = 1.0 / jnp.sqrt(jnp.float32(HD))
    keys = key_rows.reshape(CAP, KVH, HD)
    values = value_rows.reshape(CAP, KVH, HD)
    count = jnp.full((KVH,), length, dtype=jnp.int32)
    heads = jnp.arange(KVH, dtype=jnp.int32)
    slots = jnp.arange(CAP, dtype=jnp.int32)
    outputs = []
    for step in range(STEPS):
        merging = flags[step] == 1
        share = shares[step]
        target = jnp.where(merging, count - 1, count).astype(jnp.int32)
        new_keys = fresh_keys[step].reshape(KVH, HD).astype(jnp.float32)
        new_values = fresh_values[step].reshape(KVH, HD).astype(jnp.float32)
        old_keys = keys[target, heads].astype(jnp.float32)
        old_values = values[target, heads].astype(jnp.float32)
        mixed_keys = (weight[:, None] * old_keys + share[:, None] * new_keys) / (weight + share)[:, None]
        mixed_values = (weight[:, None] * old_values + share[:, None] * new_values) / (weight + share)[:, None]
        keys = keys.at[target, heads].set(jnp.where(merging[:, None], mixed_keys, new_keys).astype(jnp.bfloat16))
        values = values.at[target, heads].set(jnp.where(merging[:, None], mixed_values, new_values).astype(jnp.bfloat16))
        weight = jnp.where(merging, weight + share, share)
        count = jnp.where(merging, count, count + 1)
        query = query_rows[step].reshape(KVH, group, HD).astype(jnp.float32)
        score = jnp.einsum('gqd,kgd->gqk', query, keys.astype(jnp.float32)) * scale
        score = jnp.where(slots[None, None, :] < count[:, None, None], score, -jnp.inf)
        highest = lax.optimization_barrier(jnp.max(score, axis=2, keepdims=True))
        raw = jnp.exp(score - highest)
        total = lax.optimization_barrier(jnp.sum(raw, axis=2, keepdims=True))
        rounded = lax.optimization_barrier(raw.astype(jnp.bfloat16)).astype(jnp.float32)
        result = jnp.einsum('gqk,kgd->gqd', rounded, values.astype(jnp.float32)) / total
        outputs.append(result.astype(jnp.bfloat16).reshape(QH * HD))
    return jnp.stack(outputs)

def reference(queries, keys_new, values_new, importance, merge_flags, key_cache, value_cache, last_weight, lengths, residual, o_weight, norm_gain, expert_gate_up, expert_down, routes, route_weights):
    attended = lax.map(lambda pack: one_request(*pack), (queries, keys_new, values_new, importance, merge_flags, key_cache, value_cache, last_weight, lengths))
    rows = REQ * STEPS
    projected = jnp.dot(attended.reshape(rows, QH * HD), o_weight, preferred_element_type=jnp.float32)
    mixed = residual.reshape(rows, D).astype(jnp.float32) + projected
    normed = (mixed * lax.rsqrt(lax.optimization_barrier(jnp.mean(mixed * mixed, axis=1, keepdims=True)) + EPS) * norm_gain).astype(jnp.bfloat16)
    chosen = routes.reshape(rows, TOPK)
    gates = route_weights.reshape(rows, TOPK)
    most = CAPE * N_DP * N_EP

    def one_expert(blended, expert):
        hits = chosen == expert
        gate = lax.optimization_barrier(jnp.sum(jnp.where(hits, gates, 0.0), axis=1))
        member = jnp.any(hits, axis=1)
        picked = jnp.nonzero(member, size=most, fill_value=0)[0].astype(jnp.int32)
        valid = jnp.arange(most, dtype=jnp.int32) < jnp.sum(member.astype(jnp.int32))
        inputs = normed[picked]
        both = jnp.dot(inputs, expert_gate_up[expert], preferred_element_type=jnp.float32)
        active = (jax.nn.silu(both[:, :FF]) * both[:, FF:]).astype(jnp.bfloat16)
        output = jnp.dot(active, expert_down[expert], preferred_element_type=jnp.float32).astype(jnp.bfloat16)
        term = jnp.where(valid[:, None], gate[picked][:, None] * output.astype(jnp.float32), 0.0)
        return (blended.at[picked].add(term), expert)
    blended, unused = lax.scan(one_expert, jnp.zeros((rows, D), jnp.float32), jnp.arange(EXPERTS, dtype=jnp.int32))
    layer_out = (mixed + blended).astype(jnp.bfloat16).reshape(REQ, STEPS, D)
    return (attended, layer_out)
```

```python
import functools
import math

import jax
import jax.numpy as jnp
from jax import lax
from jax.experimental import pallas as pl
from jax.experimental.pallas import tpu as pltpu
from jax.sharding import PartitionSpec as P

EPS = 1e-06
HEAD = 128
FIRST = 128
BLOCK = 16
TOGETHER = 4


def lanes(per_head, heads):
    return jnp.concatenate(
        [jnp.broadcast_to(per_head[:, g : g + 1], (per_head.shape[0], HEAD)) for g in range(heads)],
        axis=1,
    )


def attend_kernel(
    heads,
    group,
    lengths_ref,
    flags_ref,
    queries_ref,
    keys_new_ref,
    values_new_ref,
    importance_ref,
    flags_vector_ref,
    last_weight_ref,
    key_cache_ref,
    value_cache_ref,
    out_ref,
    keys_ref,
    values_ref,
    key_slots_ref,
    value_slots_ref,
    extra_keys_ref,
    extra_values_ref,
    slot_rows_ref,
    highest_ref,
    total_ref,
    summed_ref,
    slot_sem,
    first_sem,
    rest_sem,
):
    requests, slots, features = key_cache_ref.shape
    rest = slots - FIRST
    rows = 2 * group * heads
    scale = 1.0 / math.sqrt(HEAD)

    def slot_copies(r):
        start = pl.multiple_of(((lengths_ref[r] - 1) // BLOCK) * BLOCK, BLOCK)
        return (
            pltpu.make_async_copy(
                key_cache_ref.at[r, pl.ds(start, BLOCK)], key_slots_ref.at[r], slot_sem.at[0, r]
            ),
            pltpu.make_async_copy(
                value_cache_ref.at[r, pl.ds(start, BLOCK)], value_slots_ref.at[r], slot_sem.at[1, r]
            ),
        )

    def first_copies(r):
        return (
            pltpu.make_async_copy(
                key_cache_ref.at[r, pl.ds(0, FIRST)], keys_ref.at[r, pl.ds(0, FIRST)], first_sem.at[0, r]
            ),
            pltpu.make_async_copy(
                value_cache_ref.at[r, pl.ds(0, FIRST)],
                values_ref.at[r, pl.ds(0, FIRST)],
                first_sem.at[1, r],
            ),
        )

    def rest_copies(r):
        return (
            pltpu.make_async_copy(
                key_cache_ref.at[r, pl.ds(FIRST, rest)],
                keys_ref.at[r, pl.ds(FIRST, rest)],
                rest_sem.at[0, r],
            ),
            pltpu.make_async_copy(
                value_cache_ref.at[r, pl.ds(FIRST, rest)],
                values_ref.at[r, pl.ds(FIRST, rest)],
                rest_sem.at[1, r],
            ),
        )

    def start_slots(r, carry):
        for copy in slot_copies(r):
            copy.start()
        return carry

    def start_first(r, carry):
        for copy in first_copies(r):
            copy.start()
        return carry

    def start_rest(r, carry):
        @pl.when(lengths_ref[r] > FIRST)
        def _():
            for copy in rest_copies(r):
                copy.start()

        return carry

    lax.fori_loop(0, requests, start_slots, 0)
    lax.fori_loop(0, requests, start_first, 0)
    lax.fori_loop(0, requests, start_rest, 0)

    def take_slot(r, carry):
        for copy in slot_copies(r):
            copy.wait()
        inside = (lengths_ref[r] - 1) % BLOCK
        here = lax.broadcasted_iota(jnp.int32, (BLOCK, features), 0) == inside
        for which, block_ref in ((0, key_slots_ref), (1, value_slots_ref)):
            block = block_ref[r].astype(jnp.float32)
            slot_rows_ref[which, pl.ds(r, 1), :] = jnp.sum(
                jnp.where(here, block, 0.0), axis=0, keepdims=True
            )
        return carry

    lax.fori_loop(0, requests, take_slot, 0)

    weight = lanes(last_weight_ref[...], heads)
    importance = importance_ref[...]
    flags = flags_vector_ref[...]
    share0 = lanes(importance[:, :heads], heads)
    share1 = lanes(importance[:, heads:], heads)
    merge0 = lanes(flags[:, :heads], heads) == 1
    merge1 = lanes(flags[:, heads:], heads) == 1
    weight0 = jnp.where(merge0, weight + share0, share0)
    for which, new_ref, extra_ref in (
        (0, keys_new_ref, extra_keys_ref),
        (1, values_new_ref, extra_values_ref),
    ):
        new0 = new_ref[:, :features].astype(jnp.float32)
        new1 = new_ref[:, features:].astype(jnp.float32)
        slot = slot_rows_ref[which]
        blended0 = (weight * slot + share0 * new0) / (weight + share0)
        current = jnp.where(merge0, blended0, new0).astype(jnp.bfloat16).astype(jnp.float32)
        blended1 = (weight0 * current + share1 * new1) / (weight0 + share1)
        latest = jnp.where(merge1, blended1, new1).astype(jnp.bfloat16).astype(jnp.float32)
        extra_ref[0] = current
        extra_ref[1] = latest

    row = lax.broadcasted_iota(jnp.int32, (rows, 1), 0)
    row_head = row // (2 * group)
    second = (row // group) % 2 == 1

    def by_head(r, offset):
        result = jnp.zeros((rows, 1), jnp.int32)
        for g in range(heads):
            result = jnp.where(row_head == g, flags_ref[r * 2 * heads + offset + g], result)
        return result

    def per_head_rows(vector):
        return jnp.concatenate(
            [
                jnp.broadcast_to(vector[:, g * HEAD : (g + 1) * HEAD], (2 * group, HEAD))
                for g in range(heads)
            ],
            axis=0,
        )

    def block_scores(r, start, size, queries, limit):
        parts = []
        for g in range(heads):
            parts.append(
                lax.dot_general(
                    queries[g * 2 * group : (g + 1) * 2 * group],
                    keys_ref[r, start : start + size, g * HEAD : (g + 1) * HEAD],
                    (((1,), (1,)), ((), ())),
                    preferred_element_type=jnp.float32,
                )
            )
        scores = jnp.concatenate(parts, axis=0) * scale
        position = lax.broadcasted_iota(jnp.int32, (rows, size), 1) + start
        return jnp.where(position < limit, scores, -jnp.inf)

    def block_sums(r, start, size, raw):
        raw = raw.astype(jnp.bfloat16)
        return jnp.concatenate(
            [
                jnp.dot(
                    raw[g * 2 * group : (g + 1) * 2 * group],
                    values_ref[r, start : start + size, g * HEAD : (g + 1) * HEAD],
                    preferred_element_type=jnp.float32,
                )
                for g in range(heads)
            ],
            axis=0,
        )

    def rounded(raw):
        return raw.astype(jnp.bfloat16).astype(jnp.float32)

    def first_stage(turn, carry):
        for inner in range(TOGETHER):
            for copy in first_copies(turn * TOGETHER + inner):
                copy.wait()
        for inner in range(TOGETHER):
            r = turn * TOGETHER + inner
            queries = queries_ref[r]
            wide = queries.astype(jnp.float32)
            limit = lengths_ref[r] - by_head(r, 0)
            scores = block_scores(r, 0, FIRST, queries, limit)
            current = per_head_rows(extra_keys_ref[0, pl.ds(r, 1), :])
            latest = per_head_rows(extra_keys_ref[1, pl.ds(r, 1), :])
            current_score = jnp.sum(wide * current, axis=1, keepdims=True) * scale
            latest_score = jnp.sum(wide * latest, axis=1, keepdims=True) * scale
            hidden = second & (by_head(r, heads) == 1)
            current_score = jnp.where(hidden, -jnp.inf, current_score)
            latest_score = jnp.where(second, latest_score, -jnp.inf)
            highest = jnp.maximum(
                jnp.max(scores, axis=1, keepdims=True), jnp.maximum(current_score, latest_score)
            )
            raw = jnp.exp(scores - highest)
            current_raw = jnp.exp(current_score - highest)
            latest_raw = jnp.exp(latest_score - highest)
            total = jnp.sum(raw, axis=1, keepdims=True) + current_raw + latest_raw
            summed = (
                block_sums(r, 0, FIRST, raw)
                + rounded(current_raw) * per_head_rows(extra_values_ref[0, pl.ds(r, 1), :])
                + rounded(latest_raw) * per_head_rows(extra_values_ref[1, pl.ds(r, 1), :])
            )
            highest_ref[r] = jnp.broadcast_to(highest, (rows, HEAD))
            total_ref[r] = jnp.broadcast_to(total, (rows, HEAD))
            summed_ref[r] = summed
            out_ref[r] = (summed / total).astype(jnp.bfloat16)
        return carry

    lax.fori_loop(0, requests // TOGETHER, first_stage, 0)

    def rest_stage(r, carry):
        @pl.when(lengths_ref[r] > FIRST)
        def _():
            for copy in rest_copies(r):
                copy.wait()
            limit = lengths_ref[r] - by_head(r, 0)
            scores = block_scores(r, FIRST, rest, queries_ref[r], limit)
            former = highest_ref[r][:, :1]
            highest = jnp.maximum(jnp.max(scores, axis=1, keepdims=True), former)
            raw = jnp.exp(scores - highest)
            keep = jnp.exp(former - highest)
            total = total_ref[r][:, :1] * keep + jnp.sum(raw, axis=1, keepdims=True)
            summed = summed_ref[r] * keep + block_sums(r, FIRST, rest, raw)
            out_ref[r] = (summed / total).astype(jnp.bfloat16)

        return carry

    lax.fori_loop(0, requests, rest_stage, 0)


def attend(
    queries, keys_new, values_new, importance, merge_flags, key_cache, value_cache, last_weight, lengths
):
    requests, steps, query_width = queries.shape
    heads = last_weight.shape[1]
    features = keys_new.shape[2]
    slots = key_cache.shape[1]
    group = query_width // HEAD // heads
    rows = steps * group * heads
    grouped = (
        queries.reshape(requests, steps, heads, group, HEAD)
        .transpose(0, 2, 1, 3, 4)
        .reshape(requests, rows, HEAD)
    )
    vmem = pl.BlockSpec(memory_space=pltpu.VMEM)
    smem = pl.BlockSpec(memory_space=pltpu.SMEM)
    hbm = pl.BlockSpec(memory_space=pl.ANY)
    flags = merge_flags.reshape(requests, steps * heads)
    out = pl.pallas_call(
        functools.partial(attend_kernel, heads, group),
        out_shape=jax.ShapeDtypeStruct((requests, rows, HEAD), jnp.bfloat16),
        in_specs=[smem, smem] + [vmem] * 6 + [hbm, hbm],
        out_specs=vmem,
        scratch_shapes=[
            pltpu.VMEM((requests, slots, features), jnp.bfloat16),
            pltpu.VMEM((requests, slots, features), jnp.bfloat16),
            pltpu.VMEM((requests, BLOCK, features), jnp.bfloat16),
            pltpu.VMEM((requests, BLOCK, features), jnp.bfloat16),
            pltpu.VMEM((2, requests, features), jnp.float32),
            pltpu.VMEM((2, requests, features), jnp.float32),
            pltpu.VMEM((2, requests, features), jnp.float32),
            pltpu.VMEM((requests, rows, HEAD), jnp.float32),
            pltpu.VMEM((requests, rows, HEAD), jnp.float32),
            pltpu.VMEM((requests, rows, HEAD), jnp.float32),
            pltpu.SemaphoreType.DMA((2, requests)),
            pltpu.SemaphoreType.DMA((2, requests)),
            pltpu.SemaphoreType.DMA((2, requests)),
        ],
        compiler_params=pltpu.CompilerParams(vmem_limit_bytes=48 * 1024 * 1024),
        name="attend",
    )(
        lengths,
        flags.reshape(-1),
        grouped,
        keys_new.reshape(requests, steps * features),
        values_new.reshape(requests, steps * features),
        importance.reshape(requests, steps * heads),
        flags,
        last_weight,
        key_cache,
        value_cache,
    )
    return (
        out.reshape(requests, heads, steps, group, HEAD)
        .transpose(0, 2, 1, 3, 4)
        .reshape(requests, steps, query_width)
    )


def shards(
    queries,
    keys_new,
    values_new,
    importance,
    merge_flags,
    key_cache,
    value_cache,
    last_weight,
    lengths,
    residual,
    o_weight,
    norm_gain,
    expert_gate_up,
    expert_down,
    routes,
    route_weights,
):
    requests, steps, query_width = queries.shape
    members = lax.axis_size("ep")
    sources = lax.axis_size("dp") * members
    rows = requests * steps
    top_k = routes.shape[2]
    width = o_weight.shape[1]
    every = ("dp", "ep")
    chosen = lax.all_gather(routes.reshape(rows, top_k), every, axis=0)
    gates = lax.all_gather(route_weights.reshape(rows, top_k), every, axis=0)
    attended = attend(
        queries,
        keys_new,
        values_new,
        importance,
        merge_flags,
        key_cache,
        value_cache,
        last_weight,
        lengths,
    )
    spread = lax.all_to_all(
        attended.reshape(rows, members, query_width // members),
        "ep",
        split_axis=1,
        concat_axis=0,
        tiled=True,
    )
    spread = spread.reshape(members * rows, query_width // members)
    projected = lax.psum_scatter(
        jnp.dot(spread, o_weight, preferred_element_type=jnp.float32).astype(jnp.bfloat16),
        "ep",
        scatter_dimension=0,
        tiled=True,
    )
    mixed = residual.reshape(rows, width).astype(jnp.float32) + projected.astype(jnp.float32)
    normed = (
        mixed * lax.rsqrt(jnp.mean(mixed * mixed, axis=1, keepdims=True) + EPS) * norm_gain
    ).astype(jnp.bfloat16)
    tokens = lax.all_gather(normed, every, axis=0)
    capacity = max(2, 2 * rows * top_k // sources)
    hit = chosen == lax.axis_index(every)
    gate = jnp.sum(jnp.where(hit, gates, 0.0), axis=2)
    member = jnp.any(hit, axis=2)
    rank = jnp.cumsum(member.astype(jnp.int32), axis=1) - 1
    picking = (jnp.arange(capacity)[None, :, None] == rank[:, None, :]) & member[:, None, :]
    placing = picking.astype(jnp.bfloat16)
    arrived = jnp.einsum(
        "sct,std->scd", placing, tokens, preferred_element_type=jnp.float32
    ).astype(jnp.bfloat16)
    both = jnp.dot(
        arrived.reshape(sources * capacity, width),
        expert_gate_up[0],
        preferred_element_type=jnp.float32,
    )
    hidden_units = expert_down.shape[1]
    active = (jax.nn.silu(both[:, :hidden_units]) * both[:, hidden_units:]).astype(jnp.bfloat16)
    answer = jnp.dot(active, expert_down[0], preferred_element_type=jnp.float32)
    slot_gate = jnp.sum(jnp.where(picking, gate[:, None, :], 0.0), axis=2).reshape(-1, 1)
    answer = (answer * slot_gate).astype(jnp.bfloat16).reshape(sources, capacity, width)
    share = jnp.einsum(
        "sct,scd->std", placing, answer, preferred_element_type=jnp.float32
    ).astype(jnp.bfloat16)
    blended = lax.psum_scatter(
        share.reshape(sources * rows, width), every, scatter_dimension=0, tiled=True
    )
    layer_out = (mixed + blended.astype(jnp.float32)).astype(jnp.bfloat16)
    return (attended, layer_out.reshape(requests, steps, width))


def solution(mesh):
    return jax.shard_map(
        shards,
        mesh=mesh,
        in_specs=(
            P(("dp", "ep"), None, None),
            P(("dp", "ep"), None, None),
            P(("dp", "ep"), None, None),
            P(("dp", "ep"), None, None),
            P(("dp", "ep"), None, None),
            P(("dp", "ep"), None, None),
            P(("dp", "ep"), None, None),
            P(("dp", "ep"), None),
            P(("dp", "ep")),
            P(("dp", "ep"), None, None),
            P("ep", None),
            P(),
            P(("dp", "ep"), None, None),
            P(("dp", "ep"), None, None),
            P(("dp", "ep"), None, None),
            P(("dp", "ep"), None, None),
        ),
        out_specs=(P(("dp", "ep"), None, None), P(("dp", "ep"), None, None)),
        check_vma=False,
    )
```

```python
import functools
import math

import jax
import jax.numpy as jnp
from jax import lax
from jax.experimental import pallas as pl
from jax.experimental.pallas import tpu as pltpu
from jax.sharding import PartitionSpec as P

EPS = 1e-06
HEAD = 128
FIRST = 128
BLOCK = 16
TOGETHER = 4


def lanes(per_head, heads):
    return jnp.concatenate(
        [jnp.broadcast_to(per_head[:, g : g + 1], (per_head.shape[0], HEAD)) for g in range(heads)],
        axis=1,
    )


def attend_kernel(
    heads,
    group,
    lengths_ref,
    flags_ref,
    queries_ref,
    keys_new_ref,
    values_new_ref,
    importance_ref,
    flags_vector_ref,
    last_weight_ref,
    key_cache_ref,
    value_cache_ref,
    out_ref,
    keys_ref,
    values_ref,
    key_slots_ref,
    value_slots_ref,
    extra_keys_ref,
    extra_values_ref,
    slot_rows_ref,
    highest_ref,
    total_ref,
    summed_ref,
    slot_sem,
    first_sem,
    rest_sem,
):
    requests, slots, features = key_cache_ref.shape
    rest = slots - FIRST
    rows = 2 * group * heads
    scale = 1.0 / math.sqrt(HEAD)

    def slot_copies(r):
        start = pl.multiple_of(((lengths_ref[r] - 1) // BLOCK) * BLOCK, BLOCK)
        return (
            pltpu.make_async_copy(
                key_cache_ref.at[r, pl.ds(start, BLOCK)], key_slots_ref.at[r], slot_sem.at[0, r]
            ),
            pltpu.make_async_copy(
                value_cache_ref.at[r, pl.ds(start, BLOCK)], value_slots_ref.at[r], slot_sem.at[1, r]
            ),
        )

    def first_copies(r):
        return (
            pltpu.make_async_copy(
                key_cache_ref.at[r, pl.ds(0, FIRST)], keys_ref.at[r, pl.ds(0, FIRST)], first_sem.at[0, r]
            ),
            pltpu.make_async_copy(
                value_cache_ref.at[r, pl.ds(0, FIRST)],
                values_ref.at[r, pl.ds(0, FIRST)],
                first_sem.at[1, r],
            ),
        )

    def rest_copies(r):
        return (
            pltpu.make_async_copy(
                key_cache_ref.at[r, pl.ds(FIRST, rest)],
                keys_ref.at[r, pl.ds(FIRST, rest)],
                rest_sem.at[0, r],
            ),
            pltpu.make_async_copy(
                value_cache_ref.at[r, pl.ds(FIRST, rest)],
                values_ref.at[r, pl.ds(FIRST, rest)],
                rest_sem.at[1, r],
            ),
        )

    def start_slots(r, carry):
        for copy in slot_copies(r):
            copy.start()
        return carry

    def start_first(r, carry):
        for copy in first_copies(r):
            copy.start()
        return carry

    def start_rest(r, carry):
        @pl.when(lengths_ref[r] > FIRST)
        def _():
            for copy in rest_copies(r):
                copy.start()

        return carry

    lax.fori_loop(0, requests, start_slots, 0)
    lax.fori_loop(0, requests, start_first, 0)
    lax.fori_loop(0, requests, start_rest, 0)

    def take_slot(r, carry):
        for copy in slot_copies(r):
            copy.wait()
        inside = (lengths_ref[r] - 1) % BLOCK
        here = lax.broadcasted_iota(jnp.int32, (BLOCK, features), 0) == inside
        for which, block_ref in ((0, key_slots_ref), (1, value_slots_ref)):
            block = block_ref[r].astype(jnp.float32)
            slot_rows_ref[which, pl.ds(r, 1), :] = jnp.sum(
                jnp.where(here, block, 0.0), axis=0, keepdims=True
            )
        return carry

    lax.fori_loop(0, requests, take_slot, 0)

    weight = lanes(last_weight_ref[...], heads)
    importance = importance_ref[...]
    flags = flags_vector_ref[...]
    share0 = lanes(importance[:, :heads], heads)
    share1 = lanes(importance[:, heads:], heads)
    merge0 = lanes(flags[:, :heads], heads) == 1
    merge1 = lanes(flags[:, heads:], heads) == 1
    weight0 = jnp.where(merge0, weight + share0, share0)
    for which, new_ref, extra_ref in (
        (0, keys_new_ref, extra_keys_ref),
        (1, values_new_ref, extra_values_ref),
    ):
        new0 = new_ref[:, :features].astype(jnp.float32)
        new1 = new_ref[:, features:].astype(jnp.float32)
        slot = slot_rows_ref[which]
        blended0 = (weight * slot + share0 * new0) / (weight + share0)
        current = jnp.where(merge0, blended0, new0).astype(jnp.bfloat16).astype(jnp.float32)
        blended1 = (weight0 * current + share1 * new1) / (weight0 + share1)
        latest = jnp.where(merge1, blended1, new1).astype(jnp.bfloat16).astype(jnp.float32)
        extra_ref[0] = current
        extra_ref[1] = latest

    row = lax.broadcasted_iota(jnp.int32, (rows, 1), 0)
    row_head = row // (2 * group)
    second = (row // group) % 2 == 1

    def by_head(r, offset):
        result = jnp.zeros((rows, 1), jnp.int32)
        for g in range(heads):
            result = jnp.where(row_head == g, flags_ref[r * 2 * heads + offset + g], result)
        return result

    def per_head_rows(vector):
        return jnp.concatenate(
            [
                jnp.broadcast_to(vector[:, g * HEAD : (g + 1) * HEAD], (2 * group, HEAD))
                for g in range(heads)
            ],
            axis=0,
        )

    def block_scores(r, start, size, queries, limit):
        parts = []
        for g in range(heads):
            parts.append(
                lax.dot_general(
                    queries[g * 2 * group : (g + 1) * 2 * group],
                    keys_ref[r, start : start + size, g * HEAD : (g + 1) * HEAD],
                    (((1,), (1,)), ((), ())),
                    preferred_element_type=jnp.float32,
                )
            )
        scores = jnp.concatenate(parts, axis=0) * scale
        position = lax.broadcasted_iota(jnp.int32, (rows, size), 1) + start
        return jnp.where(position < limit, scores, -jnp.inf)

    def block_sums(r, start, size, raw):
        raw = raw.astype(jnp.bfloat16)
        return jnp.concatenate(
            [
                jnp.dot(
                    raw[g * 2 * group : (g + 1) * 2 * group],
                    values_ref[r, start : start + size, g * HEAD : (g + 1) * HEAD],
                    preferred_element_type=jnp.float32,
                )
                for g in range(heads)
            ],
            axis=0,
        )

    def rounded(raw):
        return raw.astype(jnp.bfloat16).astype(jnp.float32)

    def first_stage(turn, carry):
        for inner in range(TOGETHER):
            for copy in first_copies(turn * TOGETHER + inner):
                copy.wait()
        for inner in range(TOGETHER):
            r = turn * TOGETHER + inner
            queries = queries_ref[r]
            wide = queries.astype(jnp.float32)
            limit = lengths_ref[r] - by_head(r, 0)
            scores = block_scores(r, 0, FIRST, queries, limit)
            current = per_head_rows(extra_keys_ref[0, pl.ds(r, 1), :])
            latest = per_head_rows(extra_keys_ref[1, pl.ds(r, 1), :])
            current_score = jnp.sum(wide * current, axis=1, keepdims=True) * scale
            latest_score = jnp.sum(wide * latest, axis=1, keepdims=True) * scale
            hidden = second & (by_head(r, heads) == 1)
            current_score = jnp.where(hidden, -jnp.inf, current_score)
            latest_score = jnp.where(second, latest_score, -jnp.inf)
            highest = jnp.maximum(
                jnp.max(scores, axis=1, keepdims=True), jnp.maximum(current_score, latest_score)
            )
            raw = jnp.exp(scores - highest)
            current_raw = jnp.exp(current_score - highest)
            latest_raw = jnp.exp(latest_score - highest)
            total = jnp.sum(raw, axis=1, keepdims=True) + current_raw + latest_raw
            summed = (
                block_sums(r, 0, FIRST, raw)
                + rounded(current_raw) * per_head_rows(extra_values_ref[0, pl.ds(r, 1), :])
                + rounded(latest_raw) * per_head_rows(extra_values_ref[1, pl.ds(r, 1), :])
            )
            highest_ref[r] = jnp.broadcast_to(highest, (rows, HEAD))
            total_ref[r] = jnp.broadcast_to(total, (rows, HEAD))
            summed_ref[r] = summed
            out_ref[r] = (summed / total).astype(jnp.bfloat16)
        return carry

    lax.fori_loop(0, requests // TOGETHER, first_stage, 0)

    def rest_stage(r, carry):
        @pl.when(lengths_ref[r] > FIRST)
        def _():
            for copy in rest_copies(r):
                copy.wait()
            limit = lengths_ref[r] - by_head(r, 0)
            scores = block_scores(r, FIRST, rest, queries_ref[r], limit)
            former = highest_ref[r][:, :1]
            highest = jnp.maximum(jnp.max(scores, axis=1, keepdims=True), former)
            raw = jnp.exp(scores - highest)
            keep = jnp.exp(former - highest)
            total = total_ref[r][:, :1] * keep + jnp.sum(raw, axis=1, keepdims=True)
            summed = summed_ref[r] * keep + block_sums(r, FIRST, rest, raw)
            out_ref[r] = (summed / total).astype(jnp.bfloat16)

        return carry

    lax.fori_loop(0, requests, rest_stage, 0)


def attend(
    queries, keys_new, values_new, importance, merge_flags, key_cache, value_cache, last_weight, lengths
):
    requests, steps, query_width = queries.shape
    heads = last_weight.shape[1]
    features = keys_new.shape[2]
    slots = key_cache.shape[1]
    group = query_width // HEAD // heads
    rows = steps * group * heads
    grouped = (
        queries.reshape(requests, steps, heads, group, HEAD)
        .transpose(0, 2, 1, 3, 4)
        .reshape(requests, rows, HEAD)
    )
    vmem = pl.BlockSpec(memory_space=pltpu.VMEM)
    smem = pl.BlockSpec(memory_space=pltpu.SMEM)
    hbm = pl.BlockSpec(memory_space=pl.ANY)
    flags = merge_flags.reshape(requests, steps * heads)
    out = pl.pallas_call(
        functools.partial(attend_kernel, heads, group),
        out_shape=jax.ShapeDtypeStruct((requests, rows, HEAD), jnp.bfloat16),
        in_specs=[smem, smem] + [vmem] * 6 + [hbm, hbm],
        out_specs=vmem,
        scratch_shapes=[
            pltpu.VMEM((requests, slots, features), jnp.bfloat16),
            pltpu.VMEM((requests, slots, features), jnp.bfloat16),
            pltpu.VMEM((requests, BLOCK, features), jnp.bfloat16),
            pltpu.VMEM((requests, BLOCK, features), jnp.bfloat16),
            pltpu.VMEM((2, requests, features), jnp.float32),
            pltpu.VMEM((2, requests, features), jnp.float32),
            pltpu.VMEM((2, requests, features), jnp.float32),
            pltpu.VMEM((requests, rows, HEAD), jnp.float32),
            pltpu.VMEM((requests, rows, HEAD), jnp.float32),
            pltpu.VMEM((requests, rows, HEAD), jnp.float32),
            pltpu.SemaphoreType.DMA((2, requests)),
            pltpu.SemaphoreType.DMA((2, requests)),
            pltpu.SemaphoreType.DMA((2, requests)),
        ],
        compiler_params=pltpu.CompilerParams(vmem_limit_bytes=48 * 1024 * 1024),
        name="attend",
    )(
        lengths,
        flags.reshape(-1),
        grouped,
        keys_new.reshape(requests, steps * features),
        values_new.reshape(requests, steps * features),
        importance.reshape(requests, steps * heads),
        flags,
        last_weight,
        key_cache,
        value_cache,
    )
    return (
        out.reshape(requests, heads, steps, group, HEAD)
        .transpose(0, 2, 1, 3, 4)
        .reshape(requests, steps, query_width)
    )


def shards(
    queries,
    keys_new,
    values_new,
    importance,
    merge_flags,
    key_cache,
    value_cache,
    last_weight,
    lengths,
    residual,
    o_weight,
    norm_gain,
    expert_gate_up,
    expert_down,
    routes,
    route_weights,
):
    requests, steps, query_width = queries.shape
    members = lax.axis_size("ep")
    sources = lax.axis_size("dp") * members
    rows = requests * steps
    top_k = routes.shape[2]
    width = o_weight.shape[1]
    every = ("dp", "ep")
    chosen = routes.reshape(rows, top_k)
    attended = attend(
        queries,
        keys_new,
        values_new,
        importance,
        merge_flags,
        key_cache,
        value_cache,
        last_weight,
        lengths,
    )
    spread = lax.all_to_all(
        attended.reshape(rows, members, query_width // members),
        "ep",
        split_axis=1,
        concat_axis=0,
        tiled=True,
    )
    spread = spread.reshape(members * rows, query_width // members)
    terms = jnp.dot(spread, o_weight, preferred_element_type=jnp.float32).astype(jnp.bfloat16)
    terms = lax.all_to_all(
        terms.reshape(members, rows, width), "ep", split_axis=0, concat_axis=0, tiled=True
    )
    projected = jnp.sum(terms.astype(jnp.float32), axis=0)
    mixed = residual.reshape(rows, width).astype(jnp.float32) + projected
    normed = (
        mixed * lax.rsqrt(jnp.mean(mixed * mixed, axis=1, keepdims=True) + EPS) * norm_gain
    ).astype(jnp.bfloat16)
    named = jnp.pad(chosen.astype(jnp.bfloat16), ((0, 0), (0, HEAD - top_k)), constant_values=-1)
    gathered = lax.all_gather(jnp.concatenate([normed, named], axis=1), every, axis=0)
    tokens = gathered[:, :, :width]
    capacity = max(2, 2 * rows * top_k // sources)
    hit = gathered[:, :, width : width + top_k].astype(jnp.int32) == lax.axis_index(every)
    member = jnp.any(hit, axis=2)
    rank = jnp.cumsum(member.astype(jnp.int32), axis=1) - 1
    picking = (jnp.arange(capacity)[None, :, None] == rank[:, None, :]) & member[:, None, :]
    placing = picking.astype(jnp.bfloat16)
    arrived = jnp.einsum(
        "sct,std->scd", placing, tokens, preferred_element_type=jnp.float32
    ).astype(jnp.bfloat16)
    both = jnp.dot(
        arrived.reshape(sources * capacity, width),
        expert_gate_up[0],
        preferred_element_type=jnp.float32,
    )
    hidden_units = expert_down.shape[1]
    active = (jax.nn.silu(both[:, :hidden_units]) * both[:, hidden_units:]).astype(jnp.bfloat16)
    answer = jnp.dot(active, expert_down[0], preferred_element_type=jnp.float32)
    returned = lax.all_to_all(
        answer.astype(jnp.bfloat16).reshape(sources, capacity, width),
        every,
        split_axis=0,
        concat_axis=0,
        tiled=True,
    )
    sequence = jnp.arange(rows * top_k, dtype=jnp.int32)
    flat = chosen.reshape(rows * top_k)
    earlier = sequence[:, None] > sequence[None, :]
    order = jnp.sum(((flat[:, None] == flat[None, :]) & earlier).astype(jnp.int32), axis=1)
    target = flat * capacity + order
    results = returned.reshape(sources * capacity, width)[target].reshape(rows, top_k, width)
    blended = jnp.sum(route_weights.reshape(rows, top_k, 1) * results.astype(jnp.float32), axis=1)
    layer_out = (mixed + blended).astype(jnp.bfloat16)
    return (attended, layer_out.reshape(requests, steps, width))


def solution(mesh):
    return jax.shard_map(
        shards,
        mesh=mesh,
        in_specs=(
            P(("dp", "ep"), None, None),
            P(("dp", "ep"), None, None),
            P(("dp", "ep"), None, None),
            P(("dp", "ep"), None, None),
            P(("dp", "ep"), None, None),
            P(("dp", "ep"), None, None),
            P(("dp", "ep"), None, None),
            P(("dp", "ep"), None),
            P(("dp", "ep")),
            P(("dp", "ep"), None, None),
            P("ep", None),
            P(),
            P(("dp", "ep"), None, None),
            P(("dp", "ep"), None, None),
            P(("dp", "ep"), None, None),
            P(("dp", "ep"), None, None),
        ),
        out_specs=(P(("dp", "ep"), None, None), P(("dp", "ep"), None, None)),
        check_vma=False,
    )
```

```python
import functools
import math

import jax
import jax.numpy as jnp
from jax import lax
from jax.experimental import pallas as pl
from jax.experimental.pallas import tpu as pltpu
from jax.sharding import PartitionSpec as P

EPS = 1e-06
HEAD = 128
FIRST = 128
BLOCK = 16
TOGETHER = 4


def lanes(per_head, heads):
    return jnp.concatenate(
        [jnp.broadcast_to(per_head[:, g : g + 1], (per_head.shape[0], HEAD)) for g in range(heads)],
        axis=1,
    )


def attend_kernel(
    heads,
    group,
    lengths_ref,
    flags_ref,
    queries_ref,
    keys_new_ref,
    values_new_ref,
    importance_ref,
    flags_vector_ref,
    last_weight_ref,
    key_cache_ref,
    value_cache_ref,
    out_ref,
    keys_ref,
    values_ref,
    key_slots_ref,
    value_slots_ref,
    extra_keys_ref,
    extra_values_ref,
    slot_rows_ref,
    highest_ref,
    total_ref,
    summed_ref,
    slot_sem,
    first_sem,
    rest_sem,
):
    requests, slots, features = key_cache_ref.shape
    rest = slots - FIRST
    rows = 2 * group * heads
    scale = 1.0 / math.sqrt(HEAD)

    def slot_copies(r):
        start = pl.multiple_of(((lengths_ref[r] - 1) // BLOCK) * BLOCK, BLOCK)
        return (
            pltpu.make_async_copy(
                key_cache_ref.at[r, pl.ds(start, BLOCK)], key_slots_ref.at[r], slot_sem.at[0, r]
            ),
            pltpu.make_async_copy(
                value_cache_ref.at[r, pl.ds(start, BLOCK)], value_slots_ref.at[r], slot_sem.at[1, r]
            ),
        )

    def first_copies(r):
        return (
            pltpu.make_async_copy(
                key_cache_ref.at[r, pl.ds(0, FIRST)], keys_ref.at[r, pl.ds(0, FIRST)], first_sem.at[0, r]
            ),
            pltpu.make_async_copy(
                value_cache_ref.at[r, pl.ds(0, FIRST)],
                values_ref.at[r, pl.ds(0, FIRST)],
                first_sem.at[1, r],
            ),
        )

    def rest_copies(r):
        return (
            pltpu.make_async_copy(
                key_cache_ref.at[r, pl.ds(FIRST, rest)],
                keys_ref.at[r, pl.ds(FIRST, rest)],
                rest_sem.at[0, r],
            ),
            pltpu.make_async_copy(
                value_cache_ref.at[r, pl.ds(FIRST, rest)],
                values_ref.at[r, pl.ds(FIRST, rest)],
                rest_sem.at[1, r],
            ),
        )

    def start_slots(r, carry):
        for copy in slot_copies(r):
            copy.start()
        return carry

    def start_first(r, carry):
        for copy in first_copies(r):
            copy.start()
        return carry

    def start_rest(r, carry):
        @pl.when(lengths_ref[r] > FIRST)
        def _():
            for copy in rest_copies(r):
                copy.start()

        return carry

    lax.fori_loop(0, requests, start_slots, 0)
    lax.fori_loop(0, requests, start_first, 0)
    lax.fori_loop(0, requests, start_rest, 0)

    def take_slot(r, carry):
        for copy in slot_copies(r):
            copy.wait()
        inside = (lengths_ref[r] - 1) % BLOCK
        here = lax.broadcasted_iota(jnp.int32, (BLOCK, features), 0) == inside
        for which, block_ref in ((0, key_slots_ref), (1, value_slots_ref)):
            block = block_ref[r].astype(jnp.float32)
            slot_rows_ref[which, pl.ds(r, 1), :] = jnp.sum(
                jnp.where(here, block, 0.0), axis=0, keepdims=True
            )
        return carry

    lax.fori_loop(0, requests, take_slot, 0)

    weight = lanes(last_weight_ref[...], heads)
    importance = importance_ref[...]
    flags = flags_vector_ref[...]
    share0 = lanes(importance[:, :heads], heads)
    share1 = lanes(importance[:, heads:], heads)
    merge0 = lanes(flags[:, :heads], heads) == 1
    merge1 = lanes(flags[:, heads:], heads) == 1
    weight0 = jnp.where(merge0, weight + share0, share0)
    for which, new_ref, extra_ref in (
        (0, keys_new_ref, extra_keys_ref),
        (1, values_new_ref, extra_values_ref),
    ):
        new0 = new_ref[:, :features].astype(jnp.float32)
        new1 = new_ref[:, features:].astype(jnp.float32)
        slot = slot_rows_ref[which]
        blended0 = (weight * slot + share0 * new0) / (weight + share0)
        current = jnp.where(merge0, blended0, new0).astype(jnp.bfloat16).astype(jnp.float32)
        blended1 = (weight0 * current + share1 * new1) / (weight0 + share1)
        latest = jnp.where(merge1, blended1, new1).astype(jnp.bfloat16).astype(jnp.float32)
        extra_ref[0] = current
        extra_ref[1] = latest

    row = lax.broadcasted_iota(jnp.int32, (rows, 1), 0)
    row_head = row // (2 * group)
    second = (row // group) % 2 == 1

    def by_head(r, offset):
        result = jnp.zeros((rows, 1), jnp.int32)
        for g in range(heads):
            result = jnp.where(row_head == g, flags_ref[r * 2 * heads + offset + g], result)
        return result

    def per_head_rows(vector):
        return jnp.concatenate(
            [
                jnp.broadcast_to(vector[:, g * HEAD : (g + 1) * HEAD], (2 * group, HEAD))
                for g in range(heads)
            ],
            axis=0,
        )

    def block_scores(r, start, size, queries, limit):
        parts = []
        for g in range(heads):
            parts.append(
                lax.dot_general(
                    queries[g * 2 * group : (g + 1) * 2 * group],
                    keys_ref[r, start : start + size, g * HEAD : (g + 1) * HEAD],
                    (((1,), (1,)), ((), ())),
                    preferred_element_type=jnp.float32,
                )
            )
        scores = jnp.concatenate(parts, axis=0) * scale
        position = lax.broadcasted_iota(jnp.int32, (rows, size), 1) + start
        return jnp.where(position < limit, scores, -jnp.inf)

    def block_sums(r, start, size, raw):
        raw = raw.astype(jnp.bfloat16)
        return jnp.concatenate(
            [
                jnp.dot(
                    raw[g * 2 * group : (g + 1) * 2 * group],
                    values_ref[r, start : start + size, g * HEAD : (g + 1) * HEAD],
                    preferred_element_type=jnp.float32,
                )
                for g in range(heads)
            ],
            axis=0,
        )

    def rounded(raw):
        return raw.astype(jnp.bfloat16).astype(jnp.float32)

    def first_stage(turn, carry):
        for inner in range(TOGETHER):
            for copy in first_copies(turn * TOGETHER + inner):
                copy.wait()
        for inner in range(TOGETHER):
            r = turn * TOGETHER + inner
            queries = queries_ref[r]
            wide = queries.astype(jnp.float32)
            limit = lengths_ref[r] - by_head(r, 0)
            scores = block_scores(r, 0, FIRST, queries, limit)
            current = per_head_rows(extra_keys_ref[0, pl.ds(r, 1), :])
            latest = per_head_rows(extra_keys_ref[1, pl.ds(r, 1), :])
            current_score = jnp.sum(wide * current, axis=1, keepdims=True) * scale
            latest_score = jnp.sum(wide * latest, axis=1, keepdims=True) * scale
            hidden = second & (by_head(r, heads) == 1)
            current_score = jnp.where(hidden, -jnp.inf, current_score)
            latest_score = jnp.where(second, latest_score, -jnp.inf)
            highest = jnp.maximum(
                jnp.max(scores, axis=1, keepdims=True), jnp.maximum(current_score, latest_score)
            )
            raw = jnp.exp(scores - highest)
            current_raw = jnp.exp(current_score - highest)
            latest_raw = jnp.exp(latest_score - highest)
            total = jnp.sum(raw, axis=1, keepdims=True) + current_raw + latest_raw
            summed = (
                block_sums(r, 0, FIRST, raw)
                + rounded(current_raw) * per_head_rows(extra_values_ref[0, pl.ds(r, 1), :])
                + rounded(latest_raw) * per_head_rows(extra_values_ref[1, pl.ds(r, 1), :])
            )
            highest_ref[r] = jnp.broadcast_to(highest, (rows, HEAD))
            total_ref[r] = jnp.broadcast_to(total, (rows, HEAD))
            summed_ref[r] = summed
            out_ref[r] = (summed / total).astype(jnp.bfloat16)
        return carry

    lax.fori_loop(0, requests // TOGETHER, first_stage, 0)

    def rest_stage(r, carry):
        @pl.when(lengths_ref[r] > FIRST)
        def _():
            for copy in rest_copies(r):
                copy.wait()
            limit = lengths_ref[r] - by_head(r, 0)
            scores = block_scores(r, FIRST, rest, queries_ref[r], limit)
            former = highest_ref[r][:, :1]
            highest = jnp.maximum(jnp.max(scores, axis=1, keepdims=True), former)
            raw = jnp.exp(scores - highest)
            keep = jnp.exp(former - highest)
            total = total_ref[r][:, :1] * keep + jnp.sum(raw, axis=1, keepdims=True)
            summed = summed_ref[r] * keep + block_sums(r, FIRST, rest, raw)
            out_ref[r] = (summed / total).astype(jnp.bfloat16)

        return carry

    lax.fori_loop(0, requests, rest_stage, 0)


def attend(
    queries, keys_new, values_new, importance, merge_flags, key_cache, value_cache, last_weight, lengths
):
    requests, steps, query_width = queries.shape
    heads = last_weight.shape[1]
    features = keys_new.shape[2]
    slots = key_cache.shape[1]
    group = query_width // HEAD // heads
    rows = steps * group * heads
    grouped = (
        queries.reshape(requests, steps, heads, group, HEAD)
        .transpose(0, 2, 1, 3, 4)
        .reshape(requests, rows, HEAD)
    )
    vmem = pl.BlockSpec(memory_space=pltpu.VMEM)
    smem = pl.BlockSpec(memory_space=pltpu.SMEM)
    hbm = pl.BlockSpec(memory_space=pl.ANY)
    flags = merge_flags.reshape(requests, steps * heads)
    out = pl.pallas_call(
        functools.partial(attend_kernel, heads, group),
        out_shape=jax.ShapeDtypeStruct((requests, rows, HEAD), jnp.bfloat16),
        in_specs=[smem, smem] + [vmem] * 6 + [hbm, hbm],
        out_specs=vmem,
        scratch_shapes=[
            pltpu.VMEM((requests, slots, features), jnp.bfloat16),
            pltpu.VMEM((requests, slots, features), jnp.bfloat16),
            pltpu.VMEM((requests, BLOCK, features), jnp.bfloat16),
            pltpu.VMEM((requests, BLOCK, features), jnp.bfloat16),
            pltpu.VMEM((2, requests, features), jnp.float32),
            pltpu.VMEM((2, requests, features), jnp.float32),
            pltpu.VMEM((2, requests, features), jnp.float32),
            pltpu.VMEM((requests, rows, HEAD), jnp.float32),
            pltpu.VMEM((requests, rows, HEAD), jnp.float32),
            pltpu.VMEM((requests, rows, HEAD), jnp.float32),
            pltpu.SemaphoreType.DMA((2, requests)),
            pltpu.SemaphoreType.DMA((2, requests)),
            pltpu.SemaphoreType.DMA((2, requests)),
        ],
        compiler_params=pltpu.CompilerParams(vmem_limit_bytes=48 * 1024 * 1024),
        name="attend",
    )(
        lengths,
        flags.reshape(-1),
        grouped,
        keys_new.reshape(requests, steps * features),
        values_new.reshape(requests, steps * features),
        importance.reshape(requests, steps * heads),
        flags,
        last_weight,
        key_cache,
        value_cache,
    )
    return (
        out.reshape(requests, heads, steps, group, HEAD)
        .transpose(0, 2, 1, 3, 4)
        .reshape(requests, steps, query_width)
    )


def shards(
    queries,
    keys_new,
    values_new,
    importance,
    merge_flags,
    key_cache,
    value_cache,
    last_weight,
    lengths,
    residual,
    o_weight,
    norm_gain,
    expert_gate_up,
    expert_down,
    routes,
    route_weights,
):
    requests, steps, query_width = queries.shape
    members = lax.axis_size("ep")
    sources = lax.axis_size("dp") * members
    rows = requests * steps
    top_k = routes.shape[2]
    width = o_weight.shape[1]
    every = ("dp", "ep")
    chosen = routes.reshape(rows, top_k)
    attended = attend(
        queries,
        keys_new,
        values_new,
        importance,
        merge_flags,
        key_cache,
        value_cache,
        last_weight,
        lengths,
    )
    spread = lax.all_to_all(
        attended.reshape(rows, members, query_width // members),
        "ep",
        split_axis=1,
        concat_axis=0,
        tiled=True,
    )
    spread = spread.reshape(members * rows, query_width // members)
    terms = jnp.dot(spread, o_weight, preferred_element_type=jnp.float32).astype(jnp.bfloat16)
    terms = lax.all_to_all(
        terms.reshape(members, rows, width), "ep", split_axis=0, concat_axis=0, tiled=True
    )
    projected = jnp.sum(terms.astype(jnp.float32), axis=0)
    mixed = residual.reshape(rows, width).astype(jnp.float32) + projected
    normed = (
        mixed * lax.rsqrt(jnp.mean(mixed * mixed, axis=1, keepdims=True) + EPS) * norm_gain
    ).astype(jnp.bfloat16)
    capacity = max(2, 2 * rows * top_k // sources)
    sequence = jnp.arange(rows * top_k, dtype=jnp.int32)
    flat = chosen.reshape(rows * top_k)
    earlier = sequence[:, None] > sequence[None, :]
    order = jnp.sum(((flat[:, None] == flat[None, :]) & earlier).astype(jnp.int32), axis=1)
    target = flat * capacity + order
    places = jnp.arange(sources * capacity, dtype=jnp.int32)[:, None]
    placing = jnp.any((places == target[None, :]).reshape(-1, rows, top_k), axis=2)
    outgoing = jnp.dot(
        placing.astype(jnp.bfloat16), normed, preferred_element_type=jnp.float32
    ).astype(jnp.bfloat16)
    arrived = lax.all_to_all(
        outgoing.reshape(sources, capacity, width),
        every,
        split_axis=0,
        concat_axis=0,
        tiled=True,
    )
    both = jnp.dot(
        arrived.reshape(sources * capacity, width),
        expert_gate_up[0],
        preferred_element_type=jnp.float32,
    )
    hidden_units = expert_down.shape[1]
    active = (jax.nn.silu(both[:, :hidden_units]) * both[:, hidden_units:]).astype(jnp.bfloat16)
    answer = jnp.dot(active, expert_down[0], preferred_element_type=jnp.float32)
    returned = lax.all_to_all(
        answer.astype(jnp.bfloat16).reshape(sources, capacity, width),
        every,
        split_axis=0,
        concat_axis=0,
        tiled=True,
    )
    results = returned.reshape(sources * capacity, width)[target].reshape(rows, top_k, width)
    blended = jnp.sum(route_weights.reshape(rows, top_k, 1) * results.astype(jnp.float32), axis=1)
    layer_out = (mixed + blended).astype(jnp.bfloat16)
    return (attended, layer_out.reshape(requests, steps, width))


def solution(mesh):
    return jax.shard_map(
        shards,
        mesh=mesh,
        in_specs=(
            P(("dp", "ep"), None, None),
            P(("dp", "ep"), None, None),
            P(("dp", "ep"), None, None),
            P(("dp", "ep"), None, None),
            P(("dp", "ep"), None, None),
            P(("dp", "ep"), None, None),
            P(("dp", "ep"), None, None),
            P(("dp", "ep"), None),
            P(("dp", "ep")),
            P(("dp", "ep"), None, None),
            P("ep", None),
            P(),
            P(("dp", "ep"), None, None),
            P(("dp", "ep"), None, None),
            P(("dp", "ep"), None, None),
            P(("dp", "ep"), None, None),
        ),
        out_specs=(P(("dp", "ep"), None, None), P(("dp", "ep"), None, None)),
        check_vma=False,
    )
```

```python
import functools
import math

import jax
import jax.numpy as jnp
from jax import lax
from jax.experimental import pallas as pl
from jax.experimental.pallas import tpu as pltpu
from jax.sharding import PartitionSpec as P

EPS = 1e-06
HEAD = 128
FIRST = 128
BLOCK = 16
TOGETHER = 4


def lanes(per_head, heads):
    return jnp.concatenate(
        [jnp.broadcast_to(per_head[:, g : g + 1], (per_head.shape[0], HEAD)) for g in range(heads)],
        axis=1,
    )


def attend_kernel(
    heads,
    group,
    lengths_ref,
    flags_ref,
    queries_ref,
    keys_new_ref,
    values_new_ref,
    importance_ref,
    flags_vector_ref,
    last_weight_ref,
    key_cache_ref,
    value_cache_ref,
    out_ref,
    keys_ref,
    values_ref,
    key_slots_ref,
    value_slots_ref,
    extra_keys_ref,
    extra_values_ref,
    slot_rows_ref,
    highest_ref,
    total_ref,
    summed_ref,
    slot_sem,
    first_sem,
    rest_sem,
):
    requests, slots, features = key_cache_ref.shape
    rest = slots - FIRST
    rows = 2 * group * heads
    scale = 1.0 / math.sqrt(HEAD)

    def slot_copies(r):
        start = pl.multiple_of(((lengths_ref[r] - 1) // BLOCK) * BLOCK, BLOCK)
        return (
            pltpu.make_async_copy(
                key_cache_ref.at[r, pl.ds(start, BLOCK)], key_slots_ref.at[r], slot_sem.at[0, r]
            ),
            pltpu.make_async_copy(
                value_cache_ref.at[r, pl.ds(start, BLOCK)], value_slots_ref.at[r], slot_sem.at[1, r]
            ),
        )

    def first_copies(r):
        return (
            pltpu.make_async_copy(
                key_cache_ref.at[r, pl.ds(0, FIRST)], keys_ref.at[r, pl.ds(0, FIRST)], first_sem.at[0, r]
            ),
            pltpu.make_async_copy(
                value_cache_ref.at[r, pl.ds(0, FIRST)],
                values_ref.at[r, pl.ds(0, FIRST)],
                first_sem.at[1, r],
            ),
        )

    def rest_copies(r):
        return (
            pltpu.make_async_copy(
                key_cache_ref.at[r, pl.ds(FIRST, rest)],
                keys_ref.at[r, pl.ds(FIRST, rest)],
                rest_sem.at[0, r],
            ),
            pltpu.make_async_copy(
                value_cache_ref.at[r, pl.ds(FIRST, rest)],
                values_ref.at[r, pl.ds(FIRST, rest)],
                rest_sem.at[1, r],
            ),
        )

    def start_slots(r, carry):
        for copy in slot_copies(r):
            copy.start()
        return carry

    def start_first(r, carry):
        for copy in first_copies(r):
            copy.start()
        return carry

    def start_rest(r, carry):
        @pl.when(lengths_ref[r] > FIRST)
        def _():
            for copy in rest_copies(r):
                copy.start()

        return carry

    lax.fori_loop(0, requests, start_slots, 0)
    lax.fori_loop(0, requests, start_first, 0)
    lax.fori_loop(0, requests, start_rest, 0)

    def take_slot(r, carry):
        for copy in slot_copies(r):
            copy.wait()
        inside = (lengths_ref[r] - 1) % BLOCK
        here = lax.broadcasted_iota(jnp.int32, (BLOCK, features), 0) == inside
        for which, block_ref in ((0, key_slots_ref), (1, value_slots_ref)):
            block = block_ref[r].astype(jnp.float32)
            slot_rows_ref[which, pl.ds(r, 1), :] = jnp.sum(
                jnp.where(here, block, 0.0), axis=0, keepdims=True
            )
        return carry

    lax.fori_loop(0, requests, take_slot, 0)

    weight = lanes(last_weight_ref[...], heads)
    importance = importance_ref[...]
    flags = flags_vector_ref[...]
    share0 = lanes(importance[:, :heads], heads)
    share1 = lanes(importance[:, heads:], heads)
    merge0 = lanes(flags[:, :heads], heads) == 1
    merge1 = lanes(flags[:, heads:], heads) == 1
    weight0 = jnp.where(merge0, weight + share0, share0)
    for which, new_ref, extra_ref in (
        (0, keys_new_ref, extra_keys_ref),
        (1, values_new_ref, extra_values_ref),
    ):
        new0 = new_ref[:, :features].astype(jnp.float32)
        new1 = new_ref[:, features:].astype(jnp.float32)
        slot = slot_rows_ref[which]
        blended0 = (weight * slot + share0 * new0) / (weight + share0)
        current = jnp.where(merge0, blended0, new0).astype(jnp.bfloat16).astype(jnp.float32)
        blended1 = (weight0 * current + share1 * new1) / (weight0 + share1)
        latest = jnp.where(merge1, blended1, new1).astype(jnp.bfloat16).astype(jnp.float32)
        extra_ref[0] = current
        extra_ref[1] = latest

    row = lax.broadcasted_iota(jnp.int32, (rows, 1), 0)
    row_head = row // (2 * group)
    second = (row // group) % 2 == 1

    def by_head(r, offset):
        result = jnp.zeros((rows, 1), jnp.int32)
        for g in range(heads):
            result = jnp.where(row_head == g, flags_ref[r * 2 * heads + offset + g], result)
        return result

    def per_head_rows(vector):
        return jnp.concatenate(
            [
                jnp.broadcast_to(vector[:, g * HEAD : (g + 1) * HEAD], (2 * group, HEAD))
                for g in range(heads)
            ],
            axis=0,
        )

    def block_scores(r, start, size, queries, limit):
        parts = []
        for g in range(heads):
            parts.append(
                lax.dot_general(
                    queries[g * 2 * group : (g + 1) * 2 * group],
                    keys_ref[r, start : start + size, g * HEAD : (g + 1) * HEAD],
                    (((1,), (1,)), ((), ())),
                    preferred_element_type=jnp.float32,
                )
            )
        scores = jnp.concatenate(parts, axis=0) * scale
        position = lax.broadcasted_iota(jnp.int32, (rows, size), 1) + start
        return jnp.where(position < limit, scores, -jnp.inf)

    def block_sums(r, start, size, raw):
        raw = raw.astype(jnp.bfloat16)
        return jnp.concatenate(
            [
                jnp.dot(
                    raw[g * 2 * group : (g + 1) * 2 * group],
                    values_ref[r, start : start + size, g * HEAD : (g + 1) * HEAD],
                    preferred_element_type=jnp.float32,
                )
                for g in range(heads)
            ],
            axis=0,
        )

    def rounded(raw):
        return raw.astype(jnp.bfloat16).astype(jnp.float32)

    def first_stage(turn, carry):
        for inner in range(TOGETHER):
            for copy in first_copies(turn * TOGETHER + inner):
                copy.wait()
        for inner in range(TOGETHER):
            r = turn * TOGETHER + inner
            queries = queries_ref[r]
            wide = queries.astype(jnp.float32)
            limit = lengths_ref[r] - by_head(r, 0)
            scores = block_scores(r, 0, FIRST, queries, limit)
            current = per_head_rows(extra_keys_ref[0, pl.ds(r, 1), :])
            latest = per_head_rows(extra_keys_ref[1, pl.ds(r, 1), :])
            current_score = jnp.sum(wide * current, axis=1, keepdims=True) * scale
            latest_score = jnp.sum(wide * latest, axis=1, keepdims=True) * scale
            hidden = second & (by_head(r, heads) == 1)
            current_score = jnp.where(hidden, -jnp.inf, current_score)
            latest_score = jnp.where(second, latest_score, -jnp.inf)
            highest = jnp.maximum(
                jnp.max(scores, axis=1, keepdims=True), jnp.maximum(current_score, latest_score)
            )
            raw = jnp.exp(scores - highest)
            current_raw = jnp.exp(current_score - highest)
            latest_raw = jnp.exp(latest_score - highest)
            total = jnp.sum(raw, axis=1, keepdims=True) + current_raw + latest_raw
            summed = (
                block_sums(r, 0, FIRST, raw)
                + rounded(current_raw) * per_head_rows(extra_values_ref[0, pl.ds(r, 1), :])
                + rounded(latest_raw) * per_head_rows(extra_values_ref[1, pl.ds(r, 1), :])
            )
            highest_ref[r] = jnp.broadcast_to(highest, (rows, HEAD))
            total_ref[r] = jnp.broadcast_to(total, (rows, HEAD))
            summed_ref[r] = summed
            out_ref[r] = (summed / total).astype(jnp.bfloat16)
        return carry

    lax.fori_loop(0, requests // TOGETHER, first_stage, 0)

    def rest_stage(r, carry):
        @pl.when(lengths_ref[r] > FIRST)
        def _():
            for copy in rest_copies(r):
                copy.wait()
            limit = lengths_ref[r] - by_head(r, 0)
            scores = block_scores(r, FIRST, rest, queries_ref[r], limit)
            former = highest_ref[r][:, :1]
            highest = jnp.maximum(jnp.max(scores, axis=1, keepdims=True), former)
            raw = jnp.exp(scores - highest)
            keep = jnp.exp(former - highest)
            total = total_ref[r][:, :1] * keep + jnp.sum(raw, axis=1, keepdims=True)
            summed = summed_ref[r] * keep + block_sums(r, FIRST, rest, raw)
            out_ref[r] = (summed / total).astype(jnp.bfloat16)

        return carry

    lax.fori_loop(0, requests, rest_stage, 0)


def attend(
    queries, keys_new, values_new, importance, merge_flags, key_cache, value_cache, last_weight, lengths
):
    requests, steps, query_width = queries.shape
    heads = last_weight.shape[1]
    features = keys_new.shape[2]
    slots = key_cache.shape[1]
    group = query_width // HEAD // heads
    rows = steps * group * heads
    grouped = (
        queries.reshape(requests, steps, heads, group, HEAD)
        .transpose(0, 2, 1, 3, 4)
        .reshape(requests, rows, HEAD)
    )
    vmem = pl.BlockSpec(memory_space=pltpu.VMEM)
    smem = pl.BlockSpec(memory_space=pltpu.SMEM)
    hbm = pl.BlockSpec(memory_space=pl.ANY)
    flags = merge_flags.reshape(requests, steps * heads)
    out = pl.pallas_call(
        functools.partial(attend_kernel, heads, group),
        out_shape=jax.ShapeDtypeStruct((requests, rows, HEAD), jnp.bfloat16),
        in_specs=[smem, smem] + [vmem] * 6 + [hbm, hbm],
        out_specs=vmem,
        scratch_shapes=[
            pltpu.VMEM((requests, slots, features), jnp.bfloat16),
            pltpu.VMEM((requests, slots, features), jnp.bfloat16),
            pltpu.VMEM((requests, BLOCK, features), jnp.bfloat16),
            pltpu.VMEM((requests, BLOCK, features), jnp.bfloat16),
            pltpu.VMEM((2, requests, features), jnp.float32),
            pltpu.VMEM((2, requests, features), jnp.float32),
            pltpu.VMEM((2, requests, features), jnp.float32),
            pltpu.VMEM((requests, rows, HEAD), jnp.float32),
            pltpu.VMEM((requests, rows, HEAD), jnp.float32),
            pltpu.VMEM((requests, rows, HEAD), jnp.float32),
            pltpu.SemaphoreType.DMA((2, requests)),
            pltpu.SemaphoreType.DMA((2, requests)),
            pltpu.SemaphoreType.DMA((2, requests)),
        ],
        compiler_params=pltpu.CompilerParams(vmem_limit_bytes=48 * 1024 * 1024),
        name="attend",
    )(
        lengths,
        flags.reshape(-1),
        grouped,
        keys_new.reshape(requests, steps * features),
        values_new.reshape(requests, steps * features),
        importance.reshape(requests, steps * heads),
        flags,
        last_weight,
        key_cache,
        value_cache,
    )
    return (
        out.reshape(requests, heads, steps, group, HEAD)
        .transpose(0, 2, 1, 3, 4)
        .reshape(requests, steps, query_width)
    )


def shards(
    queries,
    keys_new,
    values_new,
    importance,
    merge_flags,
    key_cache,
    value_cache,
    last_weight,
    lengths,
    residual,
    o_weight,
    norm_gain,
    expert_gate_up,
    expert_down,
    routes,
    route_weights,
):
    requests, steps, query_width = queries.shape
    members = lax.axis_size("ep")
    sources = lax.axis_size("dp") * members
    rows = requests * steps
    top_k = routes.shape[2]
    width = o_weight.shape[1]
    every = ("dp", "ep")
    chosen = routes.reshape(rows, top_k)
    attended = attend(
        queries,
        keys_new,
        values_new,
        importance,
        merge_flags,
        key_cache,
        value_cache,
        last_weight,
        lengths,
    )
    spread = lax.all_to_all(
        attended.reshape(rows, members, query_width // members),
        "ep",
        split_axis=1,
        concat_axis=0,
        tiled=True,
    )
    spread = spread.reshape(members * rows, query_width // members)
    terms = jnp.dot(spread, o_weight, preferred_element_type=jnp.float32).astype(jnp.bfloat16)
    terms = lax.all_to_all(
        terms.reshape(members, rows, width), "ep", split_axis=0, concat_axis=0, tiled=True
    )
    projected = jnp.sum(terms.astype(jnp.float32), axis=0)
    mixed = residual.reshape(rows, width).astype(jnp.float32) + projected
    normed = (
        mixed * lax.rsqrt(jnp.mean(mixed * mixed, axis=1, keepdims=True) + EPS) * norm_gain
    ).astype(jnp.bfloat16)
    capacity = max(2, 2 * rows * top_k // sources)
    sequence = jnp.arange(rows * top_k, dtype=jnp.int32)
    flat = chosen.reshape(rows * top_k)
    earlier = sequence[:, None] > sequence[None, :]
    order = jnp.sum(((flat[:, None] == flat[None, :]) & earlier).astype(jnp.int32), axis=1)
    target = flat * capacity + order
    places = jnp.arange(sources * capacity, dtype=jnp.int32)[:, None]
    placing = jnp.any((places == target[None, :]).reshape(-1, rows, top_k), axis=2)
    outgoing = jnp.dot(
        placing.astype(jnp.bfloat16), normed, preferred_element_type=jnp.float32
    ).astype(jnp.bfloat16)
    arrived = lax.all_to_all(
        outgoing.reshape(sources, capacity, width),
        every,
        split_axis=0,
        concat_axis=0,
        tiled=True,
    )
    both = jnp.dot(
        arrived.reshape(sources * capacity, width),
        expert_gate_up[0],
        preferred_element_type=jnp.float32,
    )
    hidden_units = expert_down.shape[1]
    active = (jax.nn.silu(both[:, :hidden_units]) * both[:, hidden_units:]).astype(jnp.bfloat16)
    answer = jnp.dot(active, expert_down[0], preferred_element_type=jnp.float32)
    returned = lax.all_to_all(
        answer.astype(jnp.bfloat16).reshape(sources, capacity, width),
        every,
        split_axis=0,
        concat_axis=0,
        tiled=True,
    )
    at_place = places[:, 0] == target.reshape(rows, top_k, 1)
    gate = jnp.sum(jnp.where(at_place, route_weights.reshape(rows, top_k, 1), 0.0), axis=1)
    coarse = lax.reduce_precision(gate, 8, 7)
    halves = jnp.concatenate([coarse, gate - coarse], axis=0).astype(jnp.bfloat16)
    terms = jnp.dot(
        halves, returned.reshape(sources * capacity, width), preferred_element_type=jnp.float32
    )
    blended = terms[:rows] + terms[rows:]
    layer_out = (mixed + blended).astype(jnp.bfloat16)
    return (attended, layer_out.reshape(requests, steps, width))


def solution(mesh):
    return jax.shard_map(
        shards,
        mesh=mesh,
        in_specs=(
            P(("dp", "ep"), None, None),
            P(("dp", "ep"), None, None),
            P(("dp", "ep"), None, None),
            P(("dp", "ep"), None, None),
            P(("dp", "ep"), None, None),
            P(("dp", "ep"), None, None),
            P(("dp", "ep"), None, None),
            P(("dp", "ep"), None),
            P(("dp", "ep")),
            P(("dp", "ep"), None, None),
            P("ep", None),
            P(),
            P(("dp", "ep"), None, None),
            P(("dp", "ep"), None, None),
            P(("dp", "ep"), None, None),
            P(("dp", "ep"), None, None),
        ),
        out_specs=(P(("dp", "ep"), None, None), P(("dp", "ep"), None, None)),
        check_vma=False,
    )
```
